32 devices in a mesh: groups: 2 (over y), pool: 8 (over z, core), tensor: 2 (over x).
Axes of the slice: x: 2, y: 2, z: 4, core: 2. Of those that a mesh axis runs over, the one named last changes fastest.
Arguments:
- tokens: bfloat16 [4096, 12288], P(('groups', 'pool'), 'tensor'), parts along dimension 0, may hold values from -6 to 6
- tenant_ids: int32 [4096], P(('groups', 'pool')), parts along dimension 0, may hold values from 0 to 127, as said below
- slot_table: int32 [256], P('groups'), parts along dimension 0, may hold values from 0 to 127, as said below
- value_weight: bfloat16 [12288, 1024], P('tensor', 'pool'), may hold values from -0.0546875 to 0.0546875
- low_a: bfloat16 [12288, 4096], P('tensor', ('groups', 'pool')), parts along dimension 1, may hold values from -0.0546875 to 0.0546875
- low_b: bfloat16 [4096, 1024], P(('groups', 'pool')), parts along dimension 0, may hold values from -1.5 to 1.5
- tile_data: bfloat16 [256, 4, 128, 128], P(('groups', 'pool'), 'tensor'), parts along dimension 0, may hold values from -0.5 to 0.5
- tile_pos: int32 [256, 4], P(('groups', 'pool'), 'tensor'), parts along dimension 0, may hold values from 0 to 383
Outputs:
- values: bfloat16 [4096, 1024], P(('groups', 'pool'), 'tensor'), parts along dimension 0
The draws below stay inside these ranges and needn't reach their ends.
There are 2 independent parts, one for each index of `groups`. The reference program is written for one: setup_inputs(seed, part) draws one part's arguments, and reference() takes and returns one part's arrays. A program takes and returns all parts, laid end to end along the dimension named above; an argument that names none is the same for every part. Nothing has to cross between parts.
Inputs may be any that keep to these rules, and one draw needn't show every extreme that they name: A permutation: tenant t's adapter lies in slot slot_table[t], held by pool index slot_table[t] // 16. `tenant_ids`: among the 256 tokens of one pool index, at most 64 have tenants whose slots lie with one pool index; some pool index receives exactly 64 from every pool index.
All inputs are finite; a program needn't handle non-finite values.
Results may differ from the reference program's by a relative error of at most 0.001.
Values may be sent and summed in bfloat16 or wider, within the bound.
A program may use at most 128 MiB of HBM per device.

```python
import math
import jax
import jax.numpy as jnp
from jax import lax

D = 12288
KVW = 1024
RANK = 16
TILE = 128
TPS = 2
TEN_DEV = 16
TOK_DEV = 256
TENANTS = 128
TOKENS = 2048
CAP = 64
TILES = 4
BLOCKS_DEV = 48
COLS = 8
N_POOL = 8
N_TENSOR = 2


def shared_slots(key):
    return jax.random.permutation(jax.random.fold_in(key, 7), TENANTS).astype(jnp.int32)


def draw_slot_table(key, part):
    slots = shared_slots(key)
    return slots


def owner_rows(key, busiest):
    first, second = jax.random.split(key)
    position = jnp.arange(N_POOL * CAP)
    holders = (position // CAP).astype(jnp.int32)
    scores = jax.random.randint(first, (N_POOL * CAP,), 0, 1000)
    scores = jnp.where(holders == busiest, 1000, scores)
    ranking = jnp.argsort(scores * (N_POOL * CAP) + position)
    picked = holders[ranking][:TOK_DEV - CAP]
    filled = jnp.concatenate([jnp.full((CAP,), busiest, jnp.int32), picked.astype(jnp.int32)])
    return filled[jax.random.permutation(second, TOK_DEV)]


def draw_tenant_ids(key, part):
    slots = shared_slots(key)
    key = jax.random.fold_in(key, 2)
    busiest = jax.random.randint(jax.random.fold_in(key, 3), (), 0, N_POOL).astype(jnp.int32)
    block_keys = jax.random.split(jax.random.fold_in(key, 4), N_POOL)
    holders = jax.vmap(lambda block_key: owner_rows(block_key, busiest))(block_keys).reshape(-1)
    within = jax.random.randint(jax.random.fold_in(key, 5), (TOKENS,), 0, TEN_DEV).astype(jnp.int32)
    tenant_at = jnp.argsort(slots).astype(jnp.int32)
    return jnp.take(tenant_at, holders * TEN_DEV + within).astype(jnp.int32)


def place_ends(entries, stream_key, least, top_value):
    dims = entries.shape
    spot = [jax.random.randint(jax.random.fold_in(stream_key, axis), (), 0, dims[axis]) for axis in range(len(dims))]
    entries = entries.at[tuple(spot)].set(least)
    longest = dims.index(max(dims))
    spot[longest] = (spot[longest] + 1) % dims[longest]
    return entries.at[tuple(spot)].set(top_value)


def shard_levels(own_key, shape, shards, low, high):
    def one(dim, blocks):
        heights = jax.random.uniform(jax.random.fold_in(jax.random.fold_in(own_key, 6), dim), (blocks,), jnp.float32, low / len(shards), high / len(shards))
        return jnp.repeat(jnp.exp(heights), shape[dim] // blocks).reshape((-1,) + (1,) * (len(shape) - dim - 1))

    gain = one(*shards[0])
    for cut in shards[1:]:
        gain = gain * one(*cut)
    return gain


def gaussian(key, extent, scale, reach, cuts=(), kind=jnp.bfloat16):
    result = scale * jax.random.normal(key, extent, jnp.float32)
    if cuts:
        result = result * shard_levels(key, extent, cuts, -0.22, 0.18)
    return jnp.clip(result, -reach, reach).astype(kind)


def setup_inputs(seed: int = 0, part: int = 0) -> dict:
    key_list = jax.random.split(jax.random.key(seed), 9)
    own_keys = jax.random.split(jax.random.fold_in(key_list[8], part), 9)
    return {
        "tokens": gaussian(own_keys[0], (TOKENS, D), 1.0, 6.0, ((0, 8), (1, 2))),
        "tenant_ids": draw_tenant_ids(jax.random.fold_in(jax.random.fold_in(key_list[8], part), 71), part),
        "slot_table": draw_slot_table(jax.random.fold_in(jax.random.fold_in(key_list[8], part), 71), part),
        "value_weight": gaussian(key_list[3], (D, KVW), D ** -0.5, 0.0546875, ((0, 2), (1, 8))),
        "low_a": gaussian(own_keys[4], (D, TENANTS * RANK), D ** -0.5, 0.0546875, ((0, 2), (1, 8))),
        "low_b": gaussian(own_keys[5], (TENANTS * RANK, KVW), RANK ** -0.5, 1.5, ((0, 8),)),
        "tile_data": gaussian(own_keys[6], (TENANTS, TILES, TILE, TILE), TILE ** -0.5, 0.5, ((0, 8), (1, 2))),
        "tile_pos": place_ends(jax.random.randint(own_keys[7], (TENANTS, TILES), 0, BLOCKS_DEV * COLS), jax.random.fold_in(own_keys[7], 1), 0, (BLOCKS_DEV * COLS) - 1).astype(jnp.int32),
    }


def reference(tokens, tenant_ids, slot_table, value_weight, low_a, low_b, tile_data, tile_pos):
    slot = jnp.take(slot_table, tenant_ids).astype(jnp.int32)
    base = jnp.dot(tokens, value_weight, preferred_element_type=jnp.float32)
    blocks_dev = D // TILE // N_TENSOR
    col_count = KVW // TILE
    factor_a = low_a.reshape(D, TENANTS, RANK)
    factor_b = low_b.reshape(TENANTS, RANK, KVW)
    shard_of = (jnp.arange(TILES) // TPS).astype(jnp.int32)
    block_rows = math.gcd(TOKENS, 128)
    highest = lax.Precision.HIGHEST

    def block_terms(inputs):
        feats, slots = inputs
        chosen_a = jnp.take(factor_a, slots, axis=1).astype(jnp.float32)
        coeff = jnp.einsum("nd,dnr->nr", feats.astype(jnp.float32), chosen_a, precision=highest)
        chosen_b = jnp.take(factor_b, slots, axis=0).astype(jnp.float32)
        low_rank = jnp.einsum("nr,nrk->nk", coeff, chosen_b, precision=highest)
        places = jnp.take(tile_pos, slots, axis=0).astype(jnp.int32)
        row_block = (shard_of[None, :] * blocks_dev + places // col_count).astype(jnp.int32)
        col_block = places % col_count
        blocked = feats.reshape(block_rows, D // TILE, TILE)
        picked = jnp.take_along_axis(blocked, row_block[:, :, None], axis=1).astype(jnp.float32)
        chosen_tiles = jnp.take(tile_data, slots, axis=0).astype(jnp.float32)
        products = jnp.einsum("ntf,ntfg->ntg", picked, chosen_tiles, precision=highest)
        placing = (col_block[:, :, None] == jnp.arange(col_count)[None, None, :]).astype(jnp.float32)
        sparse = jnp.einsum("ntg,ntc->ncg", products, placing, precision=highest).reshape(block_rows, KVW)
        return low_rank + sparse

    delta = lax.map(block_terms, (tokens.reshape(-1, block_rows, D), slot.reshape(-1, block_rows)))
    return (base + delta.reshape(TOKENS, KVW)).astype(jnp.bfloat16)
```

```python
import jax
import jax.numpy as jnp
from jax import lax
from jax.sharding import PartitionSpec as P

RANK = 16
CHUNKS = 2


def split3(x):
    high = lax.reduce_precision(x, 8, 7)
    rest = x - high
    mid = lax.reduce_precision(rest, 8, 7)
    low = rest - mid
    return [part.astype(jnp.bfloat16) for part in (high, mid, low)]


def local(tokens, tenant_ids, slot_table, value_weight, low_a, low_b, tile_data, tile_pos):
    local_rows, features = tokens.shape
    pool_width = lax.axis_size("pool")
    tensor_width = lax.axis_size("tensor")
    group_width = lax.axis_size("groups")
    slots_here = low_b.shape[0] // RANK
    columns = low_b.shape[1]
    own_columns = columns // tensor_width
    tile_side = tile_data.shape[-1]
    per_shard = tile_pos.shape[1]
    col_count = columns // tile_side
    capacity = 2 * local_rows // pool_width
    slot_total = slot_table.shape[0]
    bf16 = jnp.bfloat16
    f32 = jnp.float32

    def exchange(x):
        return lax.all_to_all(x, "pool", split_axis=0, concat_axis=0, tiled=True)

    share = features // group_width
    group = lax.axis_index("groups")
    part_weight = lax.dynamic_slice_in_dim(value_weight, group * share, share, axis=0)
    near_weight = lax.all_gather(part_weight, "pool", axis=1, tiled=True)

    match_table = tenant_ids[:, None] == jnp.arange(slot_total)[None, :]
    slot = jnp.sum(jnp.where(match_table, slot_table[None, :], 0), axis=1)
    holder = slot // slots_here
    local_slot = slot % slots_here
    holder_hits = (holder[:, None] == jnp.arange(pool_width)[None, :]).astype(jnp.int32)
    earlier = (jnp.arange(local_rows)[:, None] >= jnp.arange(local_rows)[None, :]).astype(bf16)
    ranks = jnp.dot(earlier, holder_hits.astype(bf16), preferred_element_type=f32).astype(jnp.int32)
    position = jnp.sum((ranks - 1) * holder_hits, axis=1)
    destination = holder * capacity + position
    places = pool_width * capacity
    hits = jnp.arange(places)[:, None] == destination[None, :]
    moving = hits.astype(bf16)
    send_tags = jnp.sum(jnp.where(hits, local_slot[None, :] + 1, 0), axis=1)

    width = features // CHUNKS
    received = []
    for chunk in range(CHUNKS):
        rows = jnp.dot(
            moving, tokens[:, chunk * width : (chunk + 1) * width], preferred_element_type=f32
        ).astype(bf16)
        received.append(exchange(rows.reshape(pool_width, capacity, width)).reshape(places, width))
    tags = exchange(send_tags.reshape(pool_width, capacity)).reshape(places)

    all_pos = lax.all_gather(tile_pos, "pool", axis=0, tiled=True)
    slot_hot = (slot[:, None] == jnp.arange(slot_total)[None, :])
    own_pos = [
        jnp.sum(jnp.where(slot_hot, all_pos[:, t][None, :], 0), axis=1) for t in range(per_shard)
    ]
    picks = []
    for t in range(per_shard):
        row_block = own_pos[t] // col_count
        picked = jnp.zeros((local_rows, tile_side), bf16)
        for block in range(features // tile_side):
            piece = tokens[:, block * tile_side : (block + 1) * tile_side]
            picked = jnp.where(row_block[:, None] == block, piece, picked)
        picks.append(picked)
    pick_rows = jnp.dot(
        moving, jnp.concatenate(picks, axis=1), preferred_element_type=f32
    ).astype(bf16)
    recv_picks = exchange(pick_rows.reshape(pool_width, capacity, -1)).reshape(places, -1)
    slot_mask = tags[:, None] == jnp.arange(1, slots_here + 1)[None, :]
    tile_mask = jnp.repeat(slot_mask, tile_side, axis=1)
    products = []
    for t in range(per_shard):
        feats = recv_picks[:, t * tile_side : (t + 1) * tile_side]
        spread = jnp.where(tile_mask, jnp.tile(feats, (1, slots_here)), jnp.zeros((), bf16))
        products.append(
            jnp.dot(
                spread, tile_data[:, t].reshape(-1, tile_side), preferred_element_type=f32
            )
        )
    home = exchange(jnp.concatenate(products, axis=1).reshape(pool_width, capacity, -1))
    own_products = jnp.take(home.reshape(places, -1), destination, axis=0)
    sparse = []
    for column in range(col_count):
        total = jnp.zeros((local_rows, tile_side), f32)
        for t in range(per_shard):
            col_block = own_pos[t] % col_count
            total = total + jnp.where(
                (col_block == column)[:, None],
                own_products[:, t * tile_side : (t + 1) * tile_side],
                0.0,
            )
        sparse.append(total)

    base = jnp.dot(
        lax.dynamic_slice_in_dim(tokens, group * share, share, axis=1),
        near_weight,
        preferred_element_type=f32,
    )
    far_weight = near_weight
    for step in range(1, group_width):
        ring = [(g, (g + 1) % group_width) for g in range(group_width)]
        far_weight = lax.ppermute(far_weight, "groups", ring)
        origin = lax.rem(group - step + group_width, group_width)
        base = base + jnp.dot(
            lax.dynamic_slice_in_dim(tokens, origin * share, share, axis=1),
            far_weight,
            preferred_element_type=f32,
        )
    summed = lax.psum_scatter(
        base + jnp.concatenate(sparse, axis=1), "tensor", scatter_dimension=1, tiled=True
    )

    own_b = lax.dynamic_slice_in_dim(
        low_b, lax.axis_index("tensor") * own_columns, own_columns, axis=1
    )
    all_b = lax.all_gather(own_b, "pool", axis=0, tiled=True)
    coeff = jnp.zeros((places, slots_here * RANK), f32)
    for chunk in range(CHUNKS):
        coeff = coeff + jnp.dot(
            received[chunk], low_a[chunk * width : (chunk + 1) * width], preferred_element_type=f32
        )
    coeff = jnp.where(jnp.repeat(slot_mask, RANK, axis=1), coeff, 0.0)
    fold = (jnp.arange(slots_here * RANK)[None, :] % RANK == jnp.arange(RANK)[:, None]).astype(f32)
    folded = lax.dot_general(
        fold, coeff, (((1,), (1,)), ((), ())), precision=lax.Precision.HIGHEST
    )
    folded = folded.reshape(RANK, pool_width, capacity).transpose(1, 0, 2)
    folded = jnp.broadcast_to(folded[:, None], (pool_width, tensor_width, RANK, capacity))
    returned = lax.all_to_all(
        folded.reshape(pool_width * tensor_width, RANK, capacity),
        ("pool", "tensor"),
        split_axis=0,
        concat_axis=0,
        tiled=True,
    )
    returned = jnp.sum(returned.reshape(pool_width, tensor_width, RANK, capacity), axis=1)
    returned = returned.transpose(0, 2, 1).reshape(places, RANK)
    own_coeff = lax.dot_general(
        hits.astype(f32), returned, (((0,), (0,)), ((), ())), precision=lax.Precision.HIGHEST
    )
    wide = jnp.where(
        jnp.repeat(slot_hot, RANK, axis=1), jnp.tile(own_coeff, (1, slot_total)), 0.0
    )
    low_rank = sum(jnp.dot(part, all_b, preferred_element_type=f32) for part in split3(wide))
    return (summed + low_rank).astype(bf16)


def solution(mesh):
    return jax.shard_map(
        local,
        mesh=mesh,
        in_specs=(
            P(("groups", "pool"), "tensor"),
            P(("groups", "pool")),
            P("groups"),
            P("tensor", "pool"),
            P("tensor", ("groups", "pool")),
            P(("groups", "pool"), None),
            P(("groups", "pool"), "tensor", None, None),
            P(("groups", "pool"), "tensor"),
        ),
        out_specs=P(("groups", "pool"), "tensor"),
        check_vma=False,
    )
```

```python
import jax
import jax.numpy as jnp
from jax import lax
from jax.sharding import PartitionSpec as P

RANK = 16
CHUNKS = 3
BF16 = jnp.bfloat16
F32 = jnp.float32


def split3(x):
    high = lax.reduce_precision(x, 8, 7)
    rest = x - high
    mid = lax.reduce_precision(rest, 8, 7)
    low = rest - mid
    return [part.astype(BF16) for part in (high, mid, low)]


def dot(a, b):
    return jnp.dot(a, b, preferred_element_type=F32)


def exchange(x):
    return lax.all_to_all(x, "pool", split_axis=0, concat_axis=0, tiled=True)


def after(x, *others):
    for other in others:
        x = x + (lax.slice(other, (0,) * other.ndim, (1,) * other.ndim).reshape((1,) * x.ndim) * 0).astype(x.dtype)
    return x


def local(tokens, tenant_ids, slot_table, value_weight, low_a, low_b, tile_data, tile_pos):
    local_rows, features = tokens.shape
    pool_width = lax.axis_size("pool")
    tensor_width = lax.axis_size("tensor")
    group_width = lax.axis_size("groups")
    me = lax.axis_index("pool")
    group = lax.axis_index("groups")
    slots_here = low_b.shape[0] // RANK
    columns = low_b.shape[1]
    own_columns = columns // tensor_width
    tile_side = tile_data.shape[-1]
    per_shard = tile_pos.shape[1]
    col_count = columns // tile_side
    slot_total = slot_table.shape[0]
    capacity = 2 * local_rows // pool_width
    main_cap = capacity * 5 // 8
    extra_cap = capacity // 2
    left_cap = capacity - main_cap
    mains = pool_width * main_cap
    extras = pool_width * extra_cap
    lefts = pool_width * left_cap

    match_table = tenant_ids[:, None] == jnp.arange(slot_total)[None, :]
    slot = jnp.sum(jnp.where(match_table, slot_table[None, :], 0), axis=1)
    holder = slot // slots_here
    holder_hits = (holder[:, None] == jnp.arange(pool_width)[None, :]).astype(jnp.int32)
    earlier = (jnp.arange(local_rows)[:, None] >= jnp.arange(local_rows)[None, :]).astype(BF16)
    ranks = dot(earlier, holder_hits.astype(BF16)).astype(jnp.int32)
    position = jnp.sum((ranks - 1) * holder_hits, axis=1)
    over = position >= main_cap
    over_rank = jnp.sum(
        jnp.where(
            (jnp.arange(local_rows)[:, None] > jnp.arange(local_rows)[None, :]) & over[None, :], 1, 0
        ),
        axis=1,
    )
    left = over & (over_rank >= extra_cap)
    main_place = jnp.where(over, -1, holder * main_cap + position)
    extra_place = jnp.where(over & ~left, over_rank, -1)
    left_place = jnp.where(left, holder * left_cap + position - main_cap, -1)
    main_hits = jnp.arange(mains)[:, None] == main_place[None, :]
    extra_hits = jnp.arange(extra_cap)[:, None] == extra_place[None, :]

    def tags_of(hits):
        return jnp.sum(jnp.where(hits, slot[None, :] + 1, 0), axis=1)

    def mask_of(tags):
        return (tags - 1 - me * slots_here)[:, None] == jnp.arange(slots_here)[None, :]

    ints = jnp.concatenate(
        [
            tags_of(main_hits),
            tags_of(extra_hits),
            tile_pos.reshape(-1),
            jnp.sum(left.astype(jnp.int32))[None],
        ]
    )
    every = lax.all_gather(ints, ("groups", "pool"), axis=0)
    any_left = jnp.sum(every[:, -1]) > 0
    mine = lax.dynamic_slice_in_dim(every, group * pool_width, pool_width, axis=0)
    main_tags = lax.dynamic_slice_in_dim(mine, me * main_cap, main_cap, axis=1).reshape(-1)
    extra_tags = mine[:, mains : mains + extra_cap].reshape(-1)
    all_pos = mine[:, mains + extra_cap : -1].reshape(slot_total, per_shard)
    main_mask = mask_of(main_tags)
    extra_mask = mask_of(extra_tags)

    share = features // group_width
    part_weight = lax.dynamic_slice_in_dim(value_weight, group * share, share, axis=0)
    near_weight = lax.all_gather(part_weight, "pool", axis=1, tiled=True)

    moving = main_hits.astype(BF16)
    width = features // CHUNKS

    def rows_of(chunk):
        rows = dot(moving, tokens[:, chunk * width : (chunk + 1) * width]).astype(BF16)
        return rows.reshape(pool_width, main_cap, width)

    received = [exchange(rows_of(0))]

    slot_hot = slot[:, None] == jnp.arange(slot_total)[None, :]
    own_pos = [
        jnp.sum(jnp.where(slot_hot, all_pos[:, t][None, :], 0), axis=1) for t in range(per_shard)
    ]
    picks = []
    for t in range(per_shard):
        row_block = own_pos[t] // col_count
        picked = jnp.zeros((local_rows, tile_side), BF16)
        for block in range(features // tile_side):
            piece = tokens[:, block * tile_side : (block + 1) * tile_side]
            picked = jnp.where(row_block[:, None] == block, piece, picked)
        picks.append(picked)
    picks = jnp.concatenate(picks, axis=1)
    extra_moving = extra_hits.astype(BF16)
    extra_rows = jnp.concatenate(
        [dot(extra_moving, tokens).astype(BF16), dot(extra_moving, picks).astype(BF16)], axis=1
    )
    extra_rows = lax.all_gather(extra_rows, "pool", axis=0, tiled=True)
    pick_rows = dot(moving, picks).astype(BF16).reshape(pool_width, main_cap, -1)
    main_picks = exchange(after(pick_rows, received[0])).reshape(mains, -1)

    received.append(exchange(after(rows_of(1), main_picks, near_weight)))

    base = dot(lax.dynamic_slice_in_dim(tokens, group * share, share, axis=1), near_weight)
    core = lax.rem(me, 2)
    half = columns // 2
    quarter = half // 2
    swap = [(p, p ^ 1) for p in range(pool_width)]
    first_pieces = []
    pieces = [
        lax.dynamic_slice_in_dim(near_weight, core * half + q * quarter, quarter, axis=1)
        for q in range(2)
    ]
    for step in range(1, group_width):
        ring = [(g, (g + 1) % group_width) for g in range(group_width)]
        origin = lax.rem(group - step + group_width, group_width)
        feats = lax.dynamic_slice_in_dim(tokens, origin * share, share, axis=1)
        pieces = [lax.ppermute(piece, "groups", ring) for piece in pieces]
        first_pieces.append(pieces[0])
        others = [lax.ppermute(piece, "pool", swap) for piece in pieces]
        own = [dot(feats, piece) for piece in pieces]
        far = [dot(feats, piece) for piece in others]
        base = base + jnp.where(
            core == 0,
            jnp.concatenate(own + far, axis=1),
            jnp.concatenate(far + own, axis=1),
        )

    def tile_products(feats, mask):
        tile_mask = jnp.repeat(mask, tile_side, axis=1)
        products = []
        for t in range(per_shard):
            wide = jnp.tile(feats[:, t * tile_side : (t + 1) * tile_side], (1, slots_here))
            wide = jnp.where(tile_mask, wide, jnp.zeros((), BF16))
            products.append(dot(wide, tile_data[:, t].reshape(-1, tile_side)))
        return jnp.concatenate(products, axis=1)

    fold = (jnp.arange(slots_here * RANK)[None, :] % RANK == jnp.arange(RANK)[:, None]).astype(F32)

    def folded(coeff, mask):
        coeff = jnp.where(jnp.repeat(mask, RANK, axis=1), coeff, 0.0)
        return lax.dot_general(
            fold, coeff, (((1,), (1,)), ((), ())), precision=lax.Precision.HIGHEST
        )

    def pick_back(hits, x):
        return lax.dot_general(
            hits.astype(F32), x, (((0,), (0,)), ((), ())), precision=lax.Precision.HIGHEST
        )

    products = jnp.concatenate(
        [
            tile_products(main_picks, main_mask).reshape(pool_width, main_cap, -1),
            tile_products(extra_rows[:, features:], extra_mask).reshape(pool_width, extra_cap, -1),
        ],
        axis=1,
    )
    home = exchange(after(products, received[1], *first_pieces))
    for chunk in range(2, CHUNKS):
        received.append(exchange(after(rows_of(chunk), home)))
    back_hits = jnp.concatenate([main_hits, extra_hits], axis=0)
    own_products = pick_back(
        back_hits,
        jnp.concatenate(
            [home[:, :main_cap].reshape(mains, -1), jnp.sum(home[:, main_cap:], axis=0)], axis=0
        ),
    )

    main_coeff = jnp.zeros((mains, slots_here * RANK), F32)
    for chunk in range(CHUNKS):
        main_coeff = main_coeff + dot(
            received[chunk].reshape(mains, width), low_a[chunk * width : (chunk + 1) * width]
        )
    extra_coeff = dot(extra_rows[:, :features], low_a)
    sent = jnp.concatenate(
        [
            folded(main_coeff, main_mask).reshape(RANK, pool_width, main_cap),
            folded(extra_coeff, extra_mask).reshape(RANK, pool_width, extra_cap),
        ],
        axis=2,
    )

    def coeff_back(x):
        x = jnp.broadcast_to(
            x.transpose(1, 0, 2)[:, None], (pool_width, tensor_width, RANK, x.shape[2])
        )
        x = lax.all_to_all(
            x.reshape(pool_width * tensor_width, RANK, -1),
            ("pool", "tensor"),
            split_axis=0,
            concat_axis=0,
            tiled=True,
        )
        x = jnp.sum(x.reshape(pool_width, tensor_width, RANK, -1), axis=1)
        return x.transpose(0, 2, 1)

    coeffs = coeff_back(sent)
    own_coeff = pick_back(
        back_hits,
        jnp.concatenate(
            [coeffs[:, :main_cap].reshape(mains, RANK), jnp.sum(coeffs[:, main_cap:], axis=0)],
            axis=0,
        ),
    )

    def leftover():
        hits = jnp.arange(lefts)[:, None] == left_place[None, :]
        chosen = hits.astype(BF16)
        rows = jnp.concatenate([dot(chosen, tokens), dot(chosen, picks)], axis=1).astype(BF16)
        rows = exchange(rows.reshape(pool_width, left_cap, -1)).reshape(lefts, -1)
        tags = exchange(tags_of(hits).reshape(pool_width, left_cap)).reshape(lefts)
        mask = mask_of(tags)
        tiles = tile_products(rows[:, features:], mask)
        tiles = exchange(tiles.reshape(pool_width, left_cap, -1)).reshape(lefts, -1)
        part = folded(dot(rows[:, :features], low_a), mask)
        part = coeff_back(part.reshape(RANK, pool_width, left_cap)).reshape(lefts, RANK)
        return pick_back(hits, tiles), pick_back(hits, part)

    def nothing():
        return (
            jnp.zeros((local_rows, per_shard * tile_side), F32),
            jnp.zeros((local_rows, RANK), F32),
        )

    more_products, more_coeff = lax.cond(any_left, leftover, nothing)
    own_products = own_products + more_products
    own_coeff = own_coeff + more_coeff

    sparse = []
    for column in range(col_count):
        total = jnp.zeros((local_rows, tile_side), F32)
        for t in range(per_shard):
            total = total + jnp.where(
                (own_pos[t] % col_count == column)[:, None],
                own_products[:, t * tile_side : (t + 1) * tile_side],
                0.0,
            )
        sparse.append(total)
    summed = lax.psum_scatter(
        base + jnp.concatenate(sparse, axis=1), "tensor", scatter_dimension=1, tiled=True
    )

    own_b = lax.dynamic_slice_in_dim(
        low_b, lax.axis_index("tensor") * own_columns, own_columns, axis=1
    )
    all_b = lax.all_gather(own_b, "pool", axis=0, tiled=True)
    wide = jnp.where(
        jnp.repeat(slot_hot, RANK, axis=1), jnp.tile(own_coeff, (1, slot_total)), 0.0
    )
    low_rank = sum(dot(part, all_b) for part in split3(wide))
    return (summed + low_rank).astype(BF16)


def solution(mesh):
    return jax.shard_map(
        local,
        mesh=mesh,
        in_specs=(
            P(("groups", "pool"), "tensor"),
            P(("groups", "pool")),
            P("groups"),
            P("tensor", "pool"),
            P("tensor", ("groups", "pool")),
            P(("groups", "pool"), None),
            P(("groups", "pool"), "tensor", None, None),
            P(("groups", "pool"), "tensor"),
        ),
        out_specs=P(("groups", "pool"), "tensor"),
        check_vma=False,
    )
```

```python
import jax
import jax.numpy as jnp
from jax import lax
from jax.sharding import PartitionSpec as P

RANK = 16
CHUNKS = 3
BF16 = jnp.bfloat16
F32 = jnp.float32


def split3(x):
    high = lax.reduce_precision(x, 8, 7)
    rest = x - high
    mid = lax.reduce_precision(rest, 8, 7)
    low = rest - mid
    return [part.astype(BF16) for part in (high, mid, low)]


def dot(a, b):
    return jnp.dot(a, b, preferred_element_type=F32)


def exchange(x):
    return lax.all_to_all(x, "pool", split_axis=0, concat_axis=0, tiled=True)


def after(x, *others):
    for other in others:
        x = x + (lax.slice(other, (0,) * other.ndim, (1,) * other.ndim).reshape((1,) * x.ndim) * 0).astype(x.dtype)
    return x


def local(tokens, tenant_ids, slot_table, value_weight, low_a, low_b, tile_data, tile_pos):
    local_rows, features = tokens.shape
    pool_width = lax.axis_size("pool")
    tensor_width = lax.axis_size("tensor")
    group_width = lax.axis_size("groups")
    me = lax.axis_index("pool")
    group = lax.axis_index("groups")
    slots_here = low_b.shape[0] // RANK
    columns = low_b.shape[1]
    own_columns = columns // tensor_width
    tile_side = tile_data.shape[-1]
    per_shard = tile_pos.shape[1]
    col_count = columns // tile_side
    slot_total = slot_table.shape[0]
    capacity = 2 * local_rows // pool_width
    main_cap = capacity * 5 // 8
    extra_cap = capacity // 2
    left_cap = capacity - main_cap
    mains = pool_width * main_cap
    extras = pool_width * extra_cap
    lefts = pool_width * left_cap

    match_table = tenant_ids[:, None] == jnp.arange(slot_total)[None, :]
    slot = jnp.sum(jnp.where(match_table, slot_table[None, :], 0), axis=1)
    holder = slot // slots_here
    holder_hits = (holder[:, None] == jnp.arange(pool_width)[None, :]).astype(jnp.int32)
    earlier = (jnp.arange(local_rows)[:, None] >= jnp.arange(local_rows)[None, :]).astype(BF16)
    ranks = dot(earlier, holder_hits.astype(BF16)).astype(jnp.int32)
    position = jnp.sum((ranks - 1) * holder_hits, axis=1)
    over = position >= main_cap
    over_rank = jnp.sum(
        jnp.where(
            (jnp.arange(local_rows)[:, None] > jnp.arange(local_rows)[None, :]) & over[None, :], 1, 0
        ),
        axis=1,
    )
    left = over & (over_rank >= extra_cap)
    main_place = jnp.where(over, -1, holder * main_cap + position)
    extra_place = jnp.where(over & ~left, over_rank, -1)
    left_place = jnp.where(left, holder * left_cap + position - main_cap, -1)
    main_hits = jnp.arange(mains)[:, None] == main_place[None, :]
    extra_hits = jnp.arange(extra_cap)[:, None] == extra_place[None, :]

    def tags_of(hits):
        return jnp.sum(jnp.where(hits, slot[None, :] + 1, 0), axis=1)

    def mask_of(tags):
        return (tags - 1 - me * slots_here)[:, None] == jnp.arange(slots_here)[None, :]

    common = jnp.concatenate(
        [tags_of(extra_hits), tile_pos.reshape(-1), jnp.sum(left.astype(jnp.int32))[None]]
    )
    every = exchange(
        jnp.concatenate(
            [
                tags_of(main_hits).reshape(pool_width, main_cap),
                jnp.broadcast_to(common[None, :], (pool_width, common.shape[0])),
            ],
            axis=1,
        )
    )
    main_tags = every[:, :main_cap].reshape(-1)
    extra_tags = every[:, main_cap : main_cap + extra_cap].reshape(-1)
    all_pos = every[:, main_cap + extra_cap : -1].reshape(slot_total, per_shard)
    left_count = jnp.sum(every[:, -1])[None]
    any_left = left_count
    for step in range(1, group_width):
        ring = [(g, (g + 1) % group_width) for g in range(group_width)]
        left_count = lax.ppermute(left_count, "groups", ring)
        any_left = any_left + left_count
    any_left = any_left[0] > 0
    main_mask = mask_of(main_tags)
    extra_mask = mask_of(extra_tags)

    share = features // group_width
    part_weight = lax.dynamic_slice_in_dim(value_weight, group * share, share, axis=0)
    near_weight = lax.all_gather(part_weight, "pool", axis=1, tiled=True)

    moving = main_hits.astype(BF16)
    width = features // CHUNKS

    def rows_of(chunk):
        rows = dot(moving, tokens[:, chunk * width : (chunk + 1) * width]).astype(BF16)
        return rows.reshape(pool_width, main_cap, width)

    received = [exchange(rows_of(0))]

    slot_hot = slot[:, None] == jnp.arange(slot_total)[None, :]
    own_pos = [
        jnp.sum(jnp.where(slot_hot, all_pos[:, t][None, :], 0), axis=1) for t in range(per_shard)
    ]
    picks = []
    for t in range(per_shard):
        row_block = own_pos[t] // col_count
        picked = jnp.zeros((local_rows, tile_side), BF16)
        for block in range(features // tile_side):
            piece = tokens[:, block * tile_side : (block + 1) * tile_side]
            picked = jnp.where(row_block[:, None] == block, piece, picked)
        picks.append(picked)
    picks = jnp.concatenate(picks, axis=1)
    extra_moving = extra_hits.astype(BF16)
    extra_rows = jnp.concatenate(
        [dot(extra_moving, tokens).astype(BF16), dot(extra_moving, picks).astype(BF16)], axis=1
    )
    extra_rows = lax.all_gather(extra_rows, "pool", axis=0, tiled=True)
    pick_rows = dot(moving, picks).astype(BF16).reshape(pool_width, main_cap, -1)
    main_picks = exchange(after(pick_rows, received[0])).reshape(mains, -1)

    received.append(exchange(after(rows_of(1), main_picks, near_weight)))

    base = dot(lax.dynamic_slice_in_dim(tokens, group * share, share, axis=1), near_weight)
    core = lax.rem(me, 2)
    half = columns // 2
    quarter = half // 2
    swap = [(p, p ^ 1) for p in range(pool_width)]
    pieces = [
        lax.dynamic_slice_in_dim(near_weight, core * half + q * quarter, quarter, axis=1)
        for q in range(2)
    ]
    for step in range(1, group_width):
        ring = [(g, (g + 1) % group_width) for g in range(group_width)]
        origin = lax.rem(group - step + group_width, group_width)
        feats = lax.dynamic_slice_in_dim(tokens, origin * share, share, axis=1)
        pieces = [lax.ppermute(piece, "groups", ring) for piece in pieces]
        others = [lax.ppermute(piece, "pool", swap) for piece in pieces]
        own = [dot(feats, piece) for piece in pieces]
        far = [dot(feats, piece) for piece in others]
        base = base + jnp.where(
            core == 0,
            jnp.concatenate(own + far, axis=1),
            jnp.concatenate(far + own, axis=1),
        )

    def tile_products(feats, mask):
        tile_mask = jnp.repeat(mask, tile_side, axis=1)
        products = []
        for t in range(per_shard):
            wide = jnp.tile(feats[:, t * tile_side : (t + 1) * tile_side], (1, slots_here))
            wide = jnp.where(tile_mask, wide, jnp.zeros((), BF16))
            products.append(dot(wide, tile_data[:, t].reshape(-1, tile_side)))
        return jnp.concatenate(products, axis=1)

    fold = (jnp.arange(slots_here * RANK)[None, :] % RANK == jnp.arange(RANK)[:, None]).astype(F32)

    def folded(coeff, mask):
        coeff = jnp.where(jnp.repeat(mask, RANK, axis=1), coeff, 0.0)
        return lax.dot_general(
            fold, coeff, (((1,), (1,)), ((), ())), precision=lax.Precision.HIGHEST
        )

    def pick_back(hits, x):
        return lax.dot_general(
            hits.astype(F32), x, (((0,), (0,)), ((), ())), precision=lax.Precision.HIGHEST
        )

    products = jnp.concatenate(
        [
            tile_products(main_picks, main_mask).reshape(pool_width, main_cap, -1),
            tile_products(extra_rows[:, features:], extra_mask).reshape(pool_width, extra_cap, -1),
        ],
        axis=1,
    )
    home = exchange(after(products, received[1]))
    for chunk in range(2, CHUNKS):
        received.append(exchange(after(rows_of(chunk), home)))
    back_hits = jnp.concatenate([main_hits, extra_hits], axis=0)
    own_products = pick_back(
        back_hits,
        jnp.concatenate(
            [home[:, :main_cap].reshape(mains, -1), jnp.sum(home[:, main_cap:], axis=0)], axis=0
        ),
    )

    main_coeff = jnp.zeros((mains, slots_here * RANK), F32)
    for chunk in range(CHUNKS):
        main_coeff = main_coeff + dot(
            received[chunk].reshape(mains, width), low_a[chunk * width : (chunk + 1) * width]
        )
    extra_coeff = dot(extra_rows[:, :features], low_a)
    sent = jnp.concatenate(
        [
            folded(main_coeff, main_mask).reshape(RANK, pool_width, main_cap),
            folded(extra_coeff, extra_mask).reshape(RANK, pool_width, extra_cap),
        ],
        axis=2,
    )

    def coeff_back(x):
        x = jnp.broadcast_to(
            x.transpose(1, 0, 2)[:, None], (pool_width, tensor_width, RANK, x.shape[2])
        )
        x = lax.all_to_all(
            x.reshape(pool_width * tensor_width, RANK, -1),
            ("pool", "tensor"),
            split_axis=0,
            concat_axis=0,
            tiled=True,
        )
        x = jnp.sum(x.reshape(pool_width, tensor_width, RANK, -1), axis=1)
        return x.transpose(0, 2, 1)

    coeffs = coeff_back(sent)
    own_coeff = pick_back(
        back_hits,
        jnp.concatenate(
            [coeffs[:, :main_cap].reshape(mains, RANK), jnp.sum(coeffs[:, main_cap:], axis=0)],
            axis=0,
        ),
    )

    def leftover():
        hits = jnp.arange(lefts)[:, None] == left_place[None, :]
        chosen = hits.astype(BF16)
        rows = jnp.concatenate([dot(chosen, tokens), dot(chosen, picks)], axis=1).astype(BF16)
        rows = exchange(rows.reshape(pool_width, left_cap, -1)).reshape(lefts, -1)
        tags = exchange(tags_of(hits).reshape(pool_width, left_cap)).reshape(lefts)
        mask = mask_of(tags)
        tiles = tile_products(rows[:, features:], mask)
        tiles = exchange(tiles.reshape(pool_width, left_cap, -1)).reshape(lefts, -1)
        part = folded(dot(rows[:, :features], low_a), mask)
        part = coeff_back(part.reshape(RANK, pool_width, left_cap)).reshape(lefts, RANK)
        return pick_back(hits, tiles), pick_back(hits, part)

    def nothing():
        return (
            jnp.zeros((local_rows, per_shard * tile_side), F32),
            jnp.zeros((local_rows, RANK), F32),
        )

    more_products, more_coeff = lax.cond(any_left, leftover, nothing)
    own_products = own_products + more_products
    own_coeff = own_coeff + more_coeff

    sparse = []
    for column in range(col_count):
        total = jnp.zeros((local_rows, tile_side), F32)
        for t in range(per_shard):
            total = total + jnp.where(
                (own_pos[t] % col_count == column)[:, None],
                own_products[:, t * tile_side : (t + 1) * tile_side],
                0.0,
            )
        sparse.append(total)
    summed = lax.psum_scatter(
        base + jnp.concatenate(sparse, axis=1), "tensor", scatter_dimension=1, tiled=True
    )

    own_b = lax.dynamic_slice_in_dim(
        low_b, lax.axis_index("tensor") * own_columns, own_columns, axis=1
    )
    all_b = lax.all_gather(own_b, "pool", axis=0, tiled=True)
    wide = jnp.where(
        jnp.repeat(slot_hot, RANK, axis=1), jnp.tile(own_coeff, (1, slot_total)), 0.0
    )
    low_rank = sum(dot(part, all_b) for part in split3(wide))
    return (summed + low_rank).astype(BF16)


def solution(mesh):
    return jax.shard_map(
        local,
        mesh=mesh,
        in_specs=(
            P(("groups", "pool"), "tensor"),
            P(("groups", "pool")),
            P("groups"),
            P("tensor", "pool"),
            P("tensor", ("groups", "pool")),
            P(("groups", "pool"), None),
            P(("groups", "pool"), "tensor", None, None),
            P(("groups", "pool"), "tensor"),
        ),
        out_specs=P(("groups", "pool"), "tensor"),
        check_vma=False,
    )
```
